512 devices in a mesh: section: 16 (over y, x), expert: 32 (over z, core).
Axes of the slice: x: 4, y: 4, z: 16, core: 2. Of those that a mesh axis runs over, the one named last changes fastest.
Arguments:
- grad_in: bfloat16 [16, 2, 1024, 3584], P('section', None, 'expert'), may hold values from -6 to 6
- fresh_grad: bfloat16 [2, 1024, 3584], P(None, 'expert'), may hold values from -6 to 6
- routes: int32 [16, 2, 2, 1024, 2], P('section', None, None, 'expert'), may hold values from 0 to 7, all different within a row; in each aligned block of 32 rows (0 to 31, 32 to 63, ..., all dimensions but the last counted through in order) at most 12 rows name the same one
- gate_weights: bfloat16 [16, 2, 2, 1024, 2], P('section', None, None, 'expert'), may hold values from 0.099609375 to 1
- saved_pre: bfloat16 [16, 2, 2, 384, 8192], P('section', None, None, None, 'expert'), may hold values from -6 to 6
- w_up: bfloat16 [16, 3584, 8192], P('section', None, 'expert'), may hold values from -0.1875 to 0.1875
- w_down: bfloat16 [16, 8192, 3584], P('section', 'expert'), may hold values from -0.09375 to 0.09375
Outputs:
- grad_out: bfloat16 [16, 2, 1024, 3584], P('section', None, 'expert')
The draws below stay inside these ranges and needn't reach their ends.
Inputs may be any that keep to these rules, and one draw needn't show every extreme that they name: `routes`: each token names 2 different experts. Among the 32 tokens of one device no expert is named more than 12 times, and in every draw some device names some expert exactly 12 times.
All inputs are finite; a program needn't handle non-finite values.
Results may differ from the reference program's by a relative error of at most 0.011.
Values may be sent and summed in bfloat16 or wider, within the bound.
No kernel may reach another device: no remote copies, remote signals or barrier semaphores. Data moves between devices by JAX's collectives and lax.ppermute only.
A program may use at most 128 MiB of HBM per device.

```python
import math
import jax
import jax.numpy as jnp
import numpy as np
from jax import lax

D = 3584
FF = 1024
SLICES = 4
TOP = 2
STEPS = 2
TOK_DEV = 32
EXPERTS = 8
FF_DEV = 256
TOKENS = 1024
CAP = 12
SECTIONS = 16
N_EXPERT = 32


def block_scale(rng, extent, cuts, low, high):
    level = 1.0
    for position, blocks in cuts:
        heights = jax.random.uniform(jax.random.fold_in(jax.random.fold_in(rng, 6), position), (blocks,), jnp.float32, low / len(cuts), high / len(cuts))
        level = level * jnp.repeat(jnp.exp(heights), extent[position] // blocks).reshape((-1,) + (1,) * (len(extent) - 1 - position))
    return level


def shared_out(rng, own, number, rows, number_of, top, limit, slope):
    sequence = jax.random.permutation(rng, number_of)
    packed, usual = shares(number_of, rows * top, limit, slope, True), shares(number_of, rows * top, limit, slope, False)
    places = jnp.arange(number_of)

    def named(tallies, rotation):
        used = int((tallies > 0).sum())
        fixed = max(1, used // 4)
        moved = fixed + (places - fixed + rotation * (used - fixed)) % max(1, number_of - fixed)
        return jnp.zeros((number_of,), jnp.int32).at[sequence[jnp.where(places < fixed, places, moved)]].set(jnp.asarray(tallies, jnp.int32))

    tallies = jnp.where(number % 4 == 0, named(packed, number // 4), named(usual, number - number // 4 - 1))
    mixed = jax.random.permutation(jax.random.fold_in(own, 3), number_of)
    donor, receiver = mixed[0:number_of // 2 * 2:2], mixed[1:number_of // 2 * 2:2]
    room = jnp.minimum(tallies[donor] - 1, limit - tallies[receiver]) // 2
    room = jnp.where((donor == sequence[0]) | (receiver == sequence[0]) | (tallies[receiver] == 0), 0, jnp.maximum(room, 0))
    moved = jax.random.randint(jax.random.fold_in(own, 4), (number_of // 2,), 0, 1 << 20) % (room + 1)
    tallies = tallies.at[donor].add(-moved).at[receiver].add(moved)
    labels = jnp.searchsorted(jnp.cumsum(tallies), jnp.arange(rows * top), side="right").astype(jnp.int32)
    table = labels.reshape(top, rows).T
    table = table[jax.random.permutation(jax.random.fold_in(own, 1), rows)]
    rotation = jax.random.randint(jax.random.fold_in(own, 2), (rows, 1), 0, top)
    return jnp.take_along_axis(table, (jnp.arange(top)[None, :] + rotation) % top, axis=1)


def shares(number_of, total, bound, skew, full):
    weights = [(1 << 20) // math.isqrt(grade ** skew) + 1 for grade in range(1, number_of + 1)]
    largest = bound if full else min(bound, max(-(-total // number_of), total * weights[0] // sum(weights)))
    least = 1 if total - largest >= number_of - 1 else 0
    counts, spare = [largest] + [least] * (number_of - 1), total - largest - least * (number_of - 1)
    while spare > 0:
        free = [i for i in range(1, number_of) if counts[i] < largest] or [i for i in range(1, number_of) if counts[i] < bound]
        mass, left = sum([weights[i] for i in free]), spare
        for i in free:
            extra = min(bound - counts[i], max(1, left * weights[i] // mass), spare)
            counts[i] = counts[i] + extra
            spare = spare - extra
    return np.array(counts)


def noise(stream_key, extent, scale, most, cuts=(), held_as=jnp.bfloat16):
    array = jax.random.normal(stream_key, extent, jnp.float32) * scale
    if len(cuts) > 0:
        array = block_scale(stream_key, extent, cuts, -0.22, 0.18) * array
    return jnp.clip(array, min=-most, max=most).astype(held_as)


def setup_inputs(seed: int = 0) -> dict:
    key_list = jax.random.split(jax.random.key(seed), 8)
    grad_in = noise(key_list[0], (SECTIONS, 2, TOKENS, D), 1.0, 6.0, ((0, 16), (2, 32)))
    fresh_grad = noise(key_list[1], (2, TOKENS, D), 1.0, 6.0, ((1, 32),))
    routes_keys = jax.random.split(jax.random.fold_in(key_list[2], 1), SECTIONS * STEPS * 2 * TOKENS // TOK_DEV)
    routes_turns = jax.random.permutation(jax.random.fold_in(key_list[2], 3), SECTIONS * STEPS * 2 * TOKENS // TOK_DEV)
    routes = jax.vmap(lambda own, number: shared_out(jax.random.fold_in(key_list[2], 2), own, number, TOK_DEV, EXPERTS, TOP, CAP, 2))(routes_keys, routes_turns).reshape((SECTIONS, STEPS, 2, TOKENS, TOP))
    gate_weights = jnp.clip(jnp.exp(math.log(1.0) - 2.306499 * jax.random.uniform(key_list[3], (SECTIONS, STEPS, 2, TOKENS, TOP), jnp.float32) ** block_scale(key_list[3], (SECTIONS, STEPS, 2, TOKENS, TOP), ((0, 16), (3, 32)), -0.2, 0.2)), 0.099609375, 1.0).astype(jnp.bfloat16)
    saved_pre = noise(key_list[4], (SECTIONS, STEPS, 2, N_EXPERT * CAP, EXPERTS * FF), 1.5, 6.0, ((0, 16), (4, 32)))
    w_up = noise(key_list[5], (SECTIONS, D, EXPERTS * FF), FF ** -0.5, 0.1875, ((0, 16), (2, 32)))
    w_down = noise(key_list[6], (SECTIONS, EXPERTS * FF, D), D ** -0.5, 0.09375, ((0, 16), (1, 32)))
    return {"grad_in": grad_in, "fresh_grad": fresh_grad, "routes": routes, "gate_weights": gate_weights, "saved_pre": saved_pre, "w_up": w_up, "w_down": w_down}


highest = lax.Precision.HIGHEST


def slot_tables(routes, gate_weights):
    experts_all = jnp.arange(EXPERTS, dtype=jnp.int32)
    matches = (routes[..., None] == experts_all).astype(jnp.int32)
    chosen = jnp.sum(matches, axis=-2)
    scaled = jnp.sum(matches.astype(jnp.float32) * gate_weights.astype(jnp.float32)[..., None], axis=-2)
    ranking = jnp.cumsum(chosen, axis=-2) - chosen
    ranking_t = jnp.swapaxes(ranking, -1, -2)
    chosen_t = jnp.swapaxes(chosen, -1, -2)
    columns = jnp.arange(CAP, dtype=jnp.int32)
    placed = ((ranking_t[..., None, :] == columns[:, None]) & (chosen_t[..., None, :] > 0)).astype(jnp.float32)
    return placed, scaled


def layer_backward(incoming, routes, gate_weights, saved_pre, w_up, w_down):
    placed, scaled = slot_tables(routes.reshape(N_EXPERT, TOK_DEV, TOP), gate_weights.reshape(N_EXPERT, TOK_DEV, TOP))
    tokens_f = incoming.astype(jnp.float32).reshape(N_EXPERT, TOK_DEV, D)
    routed = jnp.einsum('nect,nte,ntd->necd', placed, scaled, tokens_f, precision=highest).astype(jnp.bfloat16)
    slot_rows = jnp.transpose(routed, (1, 0, 2, 3)).reshape(EXPERTS, N_EXPERT * CAP, D).astype(jnp.float32)
    down_f = w_down.reshape(EXPERTS, FF, D).astype(jnp.float32)
    hidden_grad = jnp.einsum('erd,efd->erf', slot_rows, down_f, precision=highest)
    preact = jnp.transpose(saved_pre.astype(jnp.float32).reshape(N_EXPERT * CAP, EXPERTS, FF), (1, 0, 2))
    logistic = jax.nn.sigmoid(preact)
    pre_grad = (hidden_grad * logistic * (1.0 + preact * (1.0 - logistic))).astype(jnp.bfloat16)
    up_f = w_up.reshape(D, EXPERTS, SLICES, FF_DEV).astype(jnp.float32)
    pre_split = pre_grad.astype(jnp.float32).reshape(EXPERTS, N_EXPERT * CAP, SLICES, FF_DEV)
    pieces = jnp.einsum('erjf,dejf->ejrd', pre_split, up_f, precision=highest).astype(jnp.bfloat16)
    summed = jnp.sum(pieces.astype(jnp.float32), axis=1).reshape(EXPERTS, N_EXPERT, CAP, D)
    summed = jnp.transpose(summed, (1, 0, 2, 3))
    routed_sum = jnp.einsum('nect,necd->ntd', placed, summed, precision=highest)
    return (tokens_f + routed_sum).reshape(TOKENS, D).astype(jnp.bfloat16)


def reference(grad_in, fresh_grad, routes, gate_weights, saved_pre, w_up, w_down):
    current = grad_in
    result = grad_in
    for step_now in range(STEPS):
        def per_section(operands):
            grads, route_now, gate_now, pre_now, up_now, down_now = operands
            lower = layer_backward(grads[0], route_now[0], gate_now[0], pre_now[0], up_now, down_now)
            higher = layer_backward(grads[1], route_now[1], gate_now[1], pre_now[1], up_now, down_now)
            return jnp.stack([lower, higher])
        result = lax.map(per_section, (current, routes[:, step_now], gate_weights[:, step_now], saved_pre[:, step_now], w_up, w_down))
        if step_now + 1 < STEPS:
            toward_lower = jnp.concatenate([result[1:, 0], fresh_grad[0][None]], axis=0)
            toward_higher = jnp.concatenate([fresh_grad[1][None], result[:-1, 1]], axis=0)
            current = jnp.stack([toward_lower, toward_higher], axis=1)
    return result
```

```python
import jax
import jax.numpy as jnp
from jax import lax
from jax.sharding import PartitionSpec as P

SLICES = 4
STEPS = 2
INFO = 128


def from_behind(block, axis, distance):
    devices = range(lax.axis_size(axis))
    route = [(i - distance, i) for i in devices if i - distance in devices]
    return lax.ppermute(block, axis, route)


def info_columns(routes, gate_weights):
    steps, lanes, tokens, top = routes.shape
    both = jnp.concatenate([routes.astype(jnp.bfloat16), gate_weights], axis=-1)
    both = jnp.transpose(both, (1, 2, 0, 3)).reshape(lanes * tokens, steps * 2 * top)
    return jnp.pad(both, ((0, 0), (0, INFO - both.shape[1])))


def token_tables(info, saved_pre, steps, lanes, top):
    groups = lax.axis_size("expert")
    expert = (lax.axis_index("expert") // SLICES).astype(jnp.bfloat16)
    tokens = info.shape[0] // groups // lanes
    capacity = saved_pre.shape[2] // groups
    info = info[:, : steps * 2 * top].reshape(groups, lanes, tokens, steps, 2, top)
    info = jnp.transpose(info, (3, 4, 5, 0, 1, 2))
    named = info[:, 0] == expert
    gates = jnp.sum(jnp.where(named, info[:, 1].astype(jnp.float32), 0.0), axis=1)
    chosen = jnp.any(named, axis=1)
    counts = chosen.astype(jnp.int32)
    slot = jnp.cumsum(counts, axis=-1) - counts
    preact = saved_pre.astype(jnp.float32)
    logistic = jax.nn.sigmoid(preact)
    factor = logistic * (1.0 + preact * (1.0 - logistic))
    factor = factor.reshape(steps, lanes, groups, capacity, -1)
    factor = jnp.transpose(factor, (0, 2, 1, 3, 4))
    placed = jnp.zeros((steps, groups, lanes, tokens, factor.shape[-1]), jnp.float32)
    for c in range(capacity):
        placed = jnp.where((slot == c)[..., None], factor[:, :, :, c : c + 1, :], placed)
    return gates, placed


def body(grad_in, fresh_grad, routes, gate_weights, saved_pre, w_up, w_down):
    section_id = lax.axis_index("section")
    sections = lax.axis_size("section")
    groups = lax.axis_size("expert")
    _, lanes, tokens, width = grad_in.shape
    top = routes.shape[-1]
    current = grad_in[0]
    info = info_columns(routes[0], gate_weights[0])
    for step_now in range(STEPS):
        mine = current.reshape(lanes * tokens, width)
        if step_now == 0:
            gathered = lax.all_gather(
                jnp.concatenate([mine, info], axis=1), "expert", axis=0, tiled=True
            )
            gates, factor = token_tables(gathered[:, width:], saved_pre[0], STEPS, lanes, top)
            gathered = gathered[:, :width]
        else:
            gathered = lax.all_gather(mine, "expert", axis=0, tiled=True)
        routed = (gathered.astype(jnp.float32) * gates[step_now].reshape(-1, 1)).astype(jnp.bfloat16)
        hidden = jnp.einsum("rd,fd->rf", routed, w_down[0], preferred_element_type=jnp.float32)
        pre_grad = (hidden * factor[step_now].reshape(hidden.shape)).astype(jnp.bfloat16)
        partial = jnp.einsum(
            "rf,df->rd", pre_grad, w_up[0], preferred_element_type=jnp.float32
        ).astype(jnp.bfloat16)
        summed = lax.psum_scatter(partial, "expert", scatter_dimension=0, tiled=True)
        result = (mine.astype(jnp.float32) + summed.astype(jnp.float32)).astype(jnp.bfloat16)
        result = result.reshape(lanes, tokens, width)
        if step_now + 1 < STEPS:
            from_above = from_behind(result[0], "section", -1)
            from_below = from_behind(result[1], "section", 1)
            toward_lower = jnp.where(section_id == sections - 1, fresh_grad[0], from_above)
            toward_higher = jnp.where(section_id == 0, fresh_grad[1], from_below)
            current = jnp.stack([toward_lower, toward_higher])
    return result[None]


def solution(mesh):
    placed = (
        P("section", None, "expert", None),
        P(None, "expert", None),
        P("section", None, None, "expert", None),
        P("section", None, None, "expert", None),
        P("section", None, None, None, "expert"),
        P("section", None, "expert"),
        P("section", "expert", None),
    )
    return jax.shard_map(
        body,
        mesh=mesh,
        in_specs=placed,
        out_specs=P("section", None, "expert", None),
        check_vma=False,
    )
```

```python
import functools

import jax
import jax.numpy as jnp
from jax import lax
from jax.experimental import pallas as pl
from jax.experimental.pallas import tpu as pltpu
from jax.sharding import PartitionSpec as P

SLICES = 4
STEPS = 2
INFO = 128


def from_behind(block, axis, distance):
    devices = range(lax.axis_size(axis))
    route = [(i - distance, i) for i in devices if i - distance in devices]
    return lax.ppermute(block, axis, route)


def swap_cores(block):
    devices = range(lax.axis_size("expert"))
    return lax.ppermute(block, "expert", [(i, i ^ 1) for i in devices])


def hop(block, outward, only=None):
    devices = lax.axis_size("expert")
    chips = devices // 2
    route = []
    for i in range(devices):
        z, core = divmod(i, 2)
        way = 1 if core == 0 else -1
        target = (z + way) % chips
        if only and target // 2 != z // 2:
            continue
        pair = (i, 2 * target + core)
        route.append(pair if outward else pair[::-1])
    return lax.ppermute(block, "expert", route)


def row_info(routes, gate_weights):
    lanes, tokens, top = routes.shape
    experts = lax.axis_size("expert") // SLICES
    names = routes[..., None] == jnp.arange(experts, dtype=jnp.int32)
    chosen = jnp.sum(names.astype(jnp.int32), axis=2)
    rank = jnp.cumsum(chosen, axis=1) - chosen
    slots = jnp.sum(jnp.where(names, rank[:, :, None, :], 0), axis=-1)
    info = jnp.concatenate(
        [routes.astype(jnp.bfloat16), gate_weights, slots.astype(jnp.bfloat16)], axis=-1
    )
    return jnp.pad(info, ((0, 0), (0, 0), (0, INFO - 3 * top)))


def sort_matrix(info, capacity, first, second):
    lanes, rows, _ = info.shape
    tokens = rows // 2
    ids = info[..., :2].astype(jnp.float32).reshape(lanes, 2, tokens, 2)
    key = jnp.where(
        jnp.any(ids == first, axis=-1), 0, jnp.where(jnp.any(ids == second, axis=-1), 1, 2)
    )
    order = key * tokens + jnp.arange(tokens)
    rank = jnp.sum((order[..., None, :] < order[..., :, None]).astype(jnp.int32), axis=-1)
    block = jnp.arange(2)[:, None]
    rest = tokens - 2 * capacity
    place = jnp.where(
        rank < capacity,
        block * capacity + rank,
        jnp.where(
            rank < 2 * capacity,
            2 * capacity + block * capacity + rank - capacity,
            4 * capacity + block * rest + rank - 2 * capacity,
        ),
    ).reshape(lanes, 1, rows)
    return (place == jnp.arange(rows)[:, None]).astype(jnp.bfloat16)


def expert_kernel(where_ref, xa_ref, xb_ref, pre_ref, down_ref, up_ref, oa_ref, ob_ref):
    rows, width = oa_ref.shape
    chunk = 512 if width % 512 == 0 else 128
    expert = where_ref[1].astype(jnp.float32)
    slots = pre_ref.shape[2]
    gates, preacts = [], []
    for lane, x_ref in enumerate((xa_ref, xb_ref)):
        info = x_ref[:, width:].astype(jnp.float32)
        first = info[:, 0:1] == expert
        second = info[:, 1:2] == expert
        gates.append(jnp.where(first, info[:, 2:3], jnp.where(second, info[:, 3:4], 0.0)))
        slot = jnp.where(first, info[:, 4:5], jnp.where(second, info[:, 5:6], -1.0))
        column = lax.broadcasted_iota(jnp.int32, (rows, slots), 1).astype(jnp.float32)
        placed = jnp.where(slot == column, 1.0, 0.0).astype(jnp.bfloat16)
        preacts.append(
            jnp.dot(placed, pre_ref[lane, 0], preferred_element_type=jnp.float32)
        )
    preact = jnp.concatenate(preacts, axis=0)
    logistic = jax.nn.sigmoid(preact)
    factor = logistic * (1.0 + preact * (1.0 - logistic))
    hidden = jnp.zeros(factor.shape, jnp.float32)
    across = (((1,), (1,)), ((), ()))
    for start in range(0, width, chunk):
        part = jnp.concatenate(
            [
                xa_ref[:, start : start + chunk].astype(jnp.float32) * gates[0],
                xb_ref[:, start : start + chunk].astype(jnp.float32) * gates[1],
            ],
            axis=0,
        ).astype(jnp.bfloat16)
        hidden = hidden + lax.dot_general(
            part, down_ref[:, start : start + chunk], across, preferred_element_type=jnp.float32
        )
    pre_grad = (hidden * factor).astype(jnp.bfloat16)
    for start in range(0, width, chunk):
        piece = lax.dot_general(
            pre_grad, up_ref[start : start + chunk, :], across, preferred_element_type=jnp.float32
        )
        oa_ref[:, start : start + chunk] = piece[:rows].astype(oa_ref.dtype)
        ob_ref[:, start : start + chunk] = piece[rows:].astype(ob_ref.dtype)


def expert_rows(origin, expert, xa, xb, pre, down, up):
    rows = xa.shape[0]
    hidden, width = down.shape
    lanes, _, slots, _ = pre.shape

    def whole(array):
        return pl.BlockSpec(array.shape, lambda i, s: (0,) * array.ndim)

    out = jax.ShapeDtypeStruct((rows, width), jnp.bfloat16)
    return pl.pallas_call(
        expert_kernel,
        out_shape=(out, out),
        grid_spec=pltpu.PrefetchScalarGridSpec(
            num_scalar_prefetch=1,
            grid=(1,),
            in_specs=[
                whole(xa),
                whole(xb),
                pl.BlockSpec((lanes, 1, slots, hidden), lambda i, s: (0, s[0], 0, 0)),
                whole(down),
                whole(up),
            ],
            out_specs=[pl.BlockSpec((rows, width), lambda i, s: (0, 0))] * 2,
        ),
        compiler_params=pltpu.CompilerParams(vmem_limit_bytes=40 * 1024 * 1024),
        cost_estimate=pl.CostEstimate(
            flops=8 * rows * hidden * width,
            bytes_accessed=4 * hidden * width + 8 * rows * width,
            transcendentals=2 * rows * hidden,
        ),
    )(jnp.stack([origin, expert]).astype(jnp.int32), xa, xb, pre, down, up)


def add_rows(own, arrived):
    short = own.shape[0] - arrived.shape[0]
    arrived = jnp.pad(arrived.astype(jnp.float32), ((0, short), (0, 0)))
    return (own.astype(jnp.float32) + arrived).astype(jnp.bfloat16)


def body(grad_in, fresh_grad, routes, gate_weights, saved_pre, w_up, w_down):
    section_id = lax.axis_index("section")
    sections = lax.axis_size("section")
    groups = lax.axis_size("expert")
    device = lax.axis_index("expert")
    _, lanes, tokens, width = grad_in.shape
    chips, core = groups // 2, device % 2
    chip, expert = device // 2, device // SLICES
    experts = groups // SLICES
    capacity = saved_pre.shape[3] // groups
    half = chips // 2
    way = 1 - 2 * core
    outer = jnp.where(chip % 2 == 1 - core, 1, 0)
    first = (expert + way * (experts // 2 - 1 + outer)) % experts
    second = (expert + way * (experts // 2 - 2 + outer)) % experts
    sizes = [2 * tokens] * (half - 4) + [4 * capacity] * 2 + [2 * capacity] * 2

    down = jnp.concatenate([w_down[0], swap_cores(w_down[0])], axis=0)
    up = jnp.concatenate([w_up[0], swap_cores(w_up[0])], axis=1)
    pre = jnp.concatenate([saved_pre[0], swap_cores(saved_pre[0])], axis=-1)
    pre = pre.reshape(STEPS, lanes, chips, 2, capacity, pre.shape[-1])
    pre = jnp.where(core == 0, pre, pre[:, :, :, ::-1])
    pre = pre.reshape(STEPS, lanes, chips, 2 * capacity, pre.shape[-1])

    current = grad_in[0]
    for step_now in range(STEPS):
        info = row_info(routes[0, step_now], gate_weights[0, step_now])
        mine = jnp.concatenate([current, info], axis=-1)
        others = swap_cores(mine)
        other_info = others[..., width:]
        other_info = jnp.where(
            (jnp.arange(INFO) == 4) | (jnp.arange(INFO) == 5), other_info + capacity, other_info
        ).astype(jnp.bfloat16)
        both = jnp.concatenate(
            [mine, jnp.concatenate([others[..., :width], other_info], axis=-1)], axis=1
        )
        sorting = sort_matrix(both[..., width:], capacity, first, second)
        payload = jnp.einsum(
            "kpr,krd->kpd", sorting, both, preferred_element_type=jnp.float32
        ).astype(jnp.bfloat16)

        streams = [payload[lane] for lane in range(lanes)]
        partials = []
        for distance, size in enumerate(sizes, 1):
            streams = [hop(s[:size], True, only=distance == half) for s in streams]
            origin = (chip - way * distance) % chips
            partials.append(expert_rows(origin, expert, *streams, pre[step_now], down, up))
        own = expert_rows(chip, expert, mine[0], mine[1], pre[step_now], down, up)

        sums = partials[-1]
        for distance in range(half, 0, -1):
            sums = [hop(s, False, only=distance == half) for s in sums]
            if distance > 1:
                sums = [add_rows(o, s) for o, s in zip(partials[distance - 2], sums)]
        arrived = jnp.einsum(
            "kpr,kpd->krd", sorting, jnp.stack(sums), preferred_element_type=jnp.float32
        ).astype(jnp.bfloat16)
        crossed = swap_cores(arrived[:, tokens:])
        result = (
            current.astype(jnp.float32)
            + jnp.stack(own).astype(jnp.float32)
            + arrived[:, :tokens].astype(jnp.float32)
            + crossed.astype(jnp.float32)
        ).astype(jnp.bfloat16)
        if step_now + 1 < STEPS:
            from_above = from_behind(result[0], "section", -1)
            from_below = from_behind(result[1], "section", 1)
            toward_lower = jnp.where(section_id == sections - 1, fresh_grad[0], from_above)
            toward_higher = jnp.where(section_id == 0, fresh_grad[1], from_below)
            current = jnp.stack([toward_lower, toward_higher])
    return result[None]


def solution(mesh):
    placed = (
        P("section", None, "expert", None),
        P(None, "expert", None),
        P("section", None, None, "expert", None),
        P("section", None, None, "expert", None),
        P("section", None, None, None, "expert"),
        P("section", None, "expert"),
        P("section", "expert", None),
    )
    return jax.shard_map(
        body,
        mesh=mesh,
        in_specs=placed,
        out_specs=P("section", None, "expert", None),
        check_vma=False,
    )
```

```python
import jax
import jax.numpy as jnp
from jax import lax
from jax.experimental import pallas as pl
from jax.experimental.pallas import tpu as pltpu
from jax.sharding import PartitionSpec as P

SLICES = 4
STEPS = 2
INFO = 128


def from_behind(block, axis, distance):
    devices = range(lax.axis_size(axis))
    route = [(i - distance, i) for i in devices if i - distance in devices]
    return lax.ppermute(block, axis, route)


def swap_cores(block):
    devices = range(lax.axis_size("expert"))
    return lax.ppermute(block, "expert", [(i, i ^ 1) for i in devices])


def hop(block, outward, only=None):
    devices = lax.axis_size("expert")
    chips = devices // 2
    route = []
    for i in range(devices):
        z, core = divmod(i, 2)
        way = 1 if core == 0 else -1
        target = (z + way) % chips
        if only and target // 2 != z // 2:
            continue
        pair = (i, 2 * target + core)
        route.append(pair if outward else pair[::-1])
    return lax.ppermute(block, "expert", route)


def row_info(routes, gate_weights, first_slot):
    lanes, tokens, top = routes.shape
    experts = lax.axis_size("expert") // SLICES
    names = routes[..., None] == jnp.arange(experts, dtype=jnp.int32)
    chosen = jnp.sum(names.astype(jnp.int32), axis=2)
    rank = jnp.cumsum(chosen, axis=1) - chosen
    slots = jnp.sum(jnp.where(names, rank[:, :, None, :], 0), axis=-1) + first_slot
    info = jnp.concatenate(
        [routes.astype(jnp.bfloat16), gate_weights, slots.astype(jnp.bfloat16)], axis=-1
    )
    return jnp.pad(info, ((0, 0), (0, 0), (0, INFO - 3 * top)))


def sort_matrix(info, capacity, first, second):
    lanes, rows, _ = info.shape
    tokens = rows // 2
    ids = info[..., :2].astype(jnp.float32).reshape(lanes, 2, tokens, 2)
    key = jnp.where(
        jnp.any(ids == first, axis=-1), 0, jnp.where(jnp.any(ids == second, axis=-1), 1, 2)
    )
    order = key * tokens + jnp.arange(tokens)
    rank = jnp.sum((order[..., None, :] < order[..., :, None]).astype(jnp.int32), axis=-1)
    block = jnp.arange(2)[:, None]
    rest = tokens - 2 * capacity
    place = jnp.where(
        rank < capacity,
        block * capacity + rank,
        jnp.where(
            rank < 2 * capacity,
            2 * capacity + block * capacity + rank - capacity,
            4 * capacity + block * rest + rank - 2 * capacity,
        ),
    ).reshape(lanes, 1, rows)
    return (place == jnp.arange(rows)[:, None]).astype(jnp.bfloat16)


def expert_kernel(where_ref, xa_ref, xb_ref, *refs):
    (pres, downs, ups), (oa_ref, ob_ref) = (refs[0:2], refs[2:4], refs[4:6]), refs[6:]
    rows, width = oa_ref.shape
    chunk = 512 if width % 512 == 0 else 128
    expert = where_ref[1].astype(jnp.float32)
    slots = pres[0].shape[3]
    gates, placed = [], []
    for x_ref in (xa_ref, xb_ref):
        info = x_ref[:, width:].astype(jnp.float32)
        first = info[:, 0:1] == expert
        second = info[:, 1:2] == expert
        gates.append(jnp.where(first, info[:, 2:3], jnp.where(second, info[:, 3:4], 0.0)))
        slot = jnp.where(first, info[:, 4:5], jnp.where(second, info[:, 5:6], -1.0))
        column = lax.broadcasted_iota(jnp.int32, (rows, slots), 1).astype(jnp.float32)
        placed.append(jnp.where(slot == column, 1.0, 0.0).astype(jnp.bfloat16))
    across = (((1,), (1,)), ((), ()))
    hidden = [jnp.zeros((2 * rows, down.shape[0]), jnp.float32) for down in downs]
    for start in range(0, width, chunk):
        part = jnp.concatenate(
            [
                xa_ref[:, start : start + chunk].astype(jnp.float32) * gates[0],
                xb_ref[:, start : start + chunk].astype(jnp.float32) * gates[1],
            ],
            axis=0,
        ).astype(jnp.bfloat16)
        for j, down in enumerate(downs):
            hidden[j] = hidden[j] + lax.dot_general(
                part, down[:, start : start + chunk], across, preferred_element_type=jnp.float32
            )
    pre_grads = []
    for j, pre in enumerate(pres):
        preact = jnp.concatenate(
            [
                jnp.dot(placed[lane], pre[0, lane, 0], preferred_element_type=jnp.float32)
                for lane in range(2)
            ],
            axis=0,
        )
        logistic = jax.nn.sigmoid(preact)
        pre_grads.append(
            (hidden[j] * logistic * (1.0 + preact * (1.0 - logistic))).astype(jnp.bfloat16)
        )
    for start in range(0, width, chunk):
        piece = sum(
            lax.dot_general(
                g, up[start : start + chunk, :], across, preferred_element_type=jnp.float32
            )
            for g, up in zip(pre_grads, ups)
        )
        oa_ref[:, start : start + chunk] = piece[:rows].astype(oa_ref.dtype)
        ob_ref[:, start : start + chunk] = piece[rows:].astype(ob_ref.dtype)


def expert_rows(step_now, origin, expert, xa, xb, pres, downs, ups):
    rows = xa.shape[0]
    hidden, width = downs[0].shape
    _, lanes, _, slots, _ = pres[0].shape

    def whole(array):
        return pl.BlockSpec(array.shape, lambda i, s: (0,) * array.ndim)

    out = jax.ShapeDtypeStruct((rows, width), jnp.bfloat16)
    return pl.pallas_call(
        expert_kernel,
        out_shape=(out, out),
        grid_spec=pltpu.PrefetchScalarGridSpec(
            num_scalar_prefetch=1,
            grid=(1,),
            in_specs=[
                whole(xa),
                whole(xb),
                *[
                    pl.BlockSpec(
                        (1, lanes, 1, slots, hidden), lambda i, s: (step_now, 0, s[0], 0, 0)
                    )
                ]
                * 2,
                *[whole(array) for array in (*downs, *ups)],
            ],
            out_specs=[pl.BlockSpec((rows, width), lambda i, s: (0, 0))] * 2,
        ),
        compiler_params=pltpu.CompilerParams(vmem_limit_bytes=40 * 1024 * 1024),
        cost_estimate=pl.CostEstimate(
            flops=16 * rows * hidden * width,
            bytes_accessed=8 * hidden * width + 8 * rows * width,
            transcendentals=4 * rows * hidden,
        ),
    )(jnp.stack([origin, expert]).astype(jnp.int32), xa, xb, *pres, *downs, *ups)


def add_rows(own, arrived):
    short = own.shape[0] - arrived.shape[0]
    arrived = jnp.pad(arrived.astype(jnp.float32), ((0, short), (0, 0)))
    return (own.astype(jnp.float32) + arrived).astype(jnp.bfloat16)


def body(grad_in, fresh_grad, routes, gate_weights, saved_pre, w_up, w_down):
    section_id = lax.axis_index("section")
    sections = lax.axis_size("section")
    groups = lax.axis_size("expert")
    device = lax.axis_index("expert")
    _, lanes, tokens, width = grad_in.shape
    chips, core = groups // 2, lax.rem(device, 2)
    chip, expert = lax.div(device, 2), lax.div(device, SLICES)
    experts = groups // SLICES
    capacity = saved_pre.shape[3] // groups
    half = chips // 2
    way = 1 - 2 * core
    outer = jnp.where(lax.rem(chip, 2) == 1 - core, 1, 0)
    first = lax.rem(experts + expert + way * (experts // 2 - 1 + outer), experts)
    second = lax.rem(experts + expert + way * (experts // 2 - 2 + outer), experts)
    sizes = [2 * tokens] * (half - 4) + [4 * capacity] * 2 + [2 * capacity] * 2

    def with_other(block):
        return block, swap_cores(block)

    def by_chip(block):
        return block.reshape(STEPS, lanes, chips, 2 * capacity, block.shape[-1])

    current = grad_in[0]
    weights = None
    for step_now in range(STEPS):
        info = row_info(routes[0, step_now], gate_weights[0, step_now], core * capacity)
        mine = jnp.concatenate([current, info], axis=-1)
        both = jnp.concatenate([mine, swap_cores(mine)], axis=1)
        sorting = sort_matrix(both[..., width:], capacity, first, second)
        payload = jnp.einsum(
            "kpr,krd->kpd", sorting, both, preferred_element_type=jnp.float32
        ).astype(jnp.bfloat16)
        if weights is None:
            saved, down, up, payload = lax.optimization_barrier(
                (saved_pre[0], w_down[0], w_up[0], payload)
            )
            pres = [by_chip(block) for block in with_other(saved)]
            weights = pres, with_other(down), with_other(up)

        def compute(origin, xa, xb):
            return expert_rows(step_now, origin, expert, xa, xb, *weights)

        streams = [payload[lane] for lane in range(lanes)]
        own, partials = None, []
        for distance, size in enumerate(sizes, 1):
            streams = [hop(s[:size], True, only=distance == half) for s in streams]
            if distance >= 2:
                held = [lax.optimization_barrier(pair) for pair in zip(streams, partials[-1])]
                streams, partials[-1] = zip(*held)
            if distance == half - 1:
                own = compute(chip, mine[0], mine[1])
                held = [lax.optimization_barrier(pair) for pair in zip(streams, own)]
                streams, own = zip(*held)
            origin = lax.rem(chips + chip - way * distance, chips)
            partials.append(compute(origin, *streams))

        sums = partials[-1]
        for distance in range(half, 0, -1):
            sums = [hop(s, False, only=distance == half) for s in sums]
            if distance > 1:
                sums = [add_rows(o, s) for o, s in zip(partials[distance - 2], sums)]
        arrived = jnp.einsum(
            "kpr,kpd->krd", sorting, jnp.stack(sums), preferred_element_type=jnp.float32
        ).astype(jnp.bfloat16)
        crossed = swap_cores(arrived[:, tokens:])
        result = (
            current.astype(jnp.float32)
            + jnp.stack(own).astype(jnp.float32)
            + arrived[:, :tokens].astype(jnp.float32)
            + crossed.astype(jnp.float32)
        ).astype(jnp.bfloat16)
        if step_now + 1 < STEPS:
            from_above = from_behind(result[0], "section", -1)
            from_below = from_behind(result[1], "section", 1)
            toward_lower = jnp.where(section_id == sections - 1, fresh_grad[0], from_above)
            toward_higher = jnp.where(section_id == 0, fresh_grad[1], from_below)
            current = jnp.stack([toward_lower, toward_higher])
    return result[None]


def solution(mesh):
    placed = (
        P("section", None, "expert", None),
        P(None, "expert", None),
        P("section", None, None, "expert", None),
        P("section", None, None, "expert", None),
        P("section", None, None, None, "expert"),
        P("section", None, "expert"),
        P("section", "expert", None),
    )
    return jax.shard_map(
        body,
        mesh=mesh,
        in_specs=placed,
        out_specs=P("section", None, "expert", None),
        check_vma=False,
    )
```

```python
import functools

import jax
import jax.numpy as jnp
from jax import lax
from jax.experimental import pallas as pl
from jax.experimental.pallas import tpu as pltpu
from jax.sharding import PartitionSpec as P

SLICES = 4
STEPS = 2
INFO = 128


def from_behind(block, axis, distance):
    devices = range(lax.axis_size(axis))
    route = [(i - distance, i) for i in devices if i - distance in devices]
    return lax.ppermute(block, axis, route)


def swap_cores(block):
    devices = range(lax.axis_size("expert"))
    return lax.ppermute(block, "expert", [(i, i ^ 1) for i in devices])


def hop(block, outward, only=None):
    devices = lax.axis_size("expert")
    chips = devices // 2
    route = []
    for i in range(devices):
        z, core = divmod(i, 2)
        way = 1 if core == 0 else -1
        target = (z + way) % chips
        if only and target // 2 != z // 2:
            continue
        pair = (i, 2 * target + core)
        route.append(pair if outward else pair[::-1])
    return lax.ppermute(block, "expert", route)


def row_info(routes, gate_weights, first_slot):
    lanes, tokens, top = routes.shape
    experts = lax.axis_size("expert") // SLICES
    names = routes[..., None] == jnp.arange(experts, dtype=jnp.int32)
    chosen = jnp.sum(names.astype(jnp.int32), axis=2)
    rank = jnp.cumsum(chosen, axis=1) - chosen
    slots = jnp.sum(jnp.where(names, rank[:, :, None, :], 0), axis=-1) + first_slot
    info = jnp.concatenate(
        [routes.astype(jnp.bfloat16), gate_weights, slots.astype(jnp.bfloat16)], axis=-1
    )
    return jnp.pad(info, ((0, 0), (0, 0), (0, INFO - 3 * top)))


def sort_matrix(info, capacity, first, second):
    lanes, rows, _ = info.shape
    tokens = rows // 2
    ids = info[..., :2].astype(jnp.float32).reshape(lanes, 2, tokens, 2)
    key = jnp.where(
        jnp.any(ids == first, axis=-1), 0, jnp.where(jnp.any(ids == second, axis=-1), 1, 2)
    )
    order = key * tokens + jnp.arange(tokens)
    rank = jnp.sum((order[..., None, :] < order[..., :, None]).astype(jnp.int32), axis=-1)
    block = jnp.arange(2)[:, None]
    rest = tokens - 2 * capacity
    place = jnp.where(
        rank < capacity,
        block * capacity + rank,
        jnp.where(
            rank < 2 * capacity,
            2 * capacity + block * capacity + rank - capacity,
            4 * capacity + block * rest + rank - 2 * capacity,
        ),
    ).reshape(lanes, 1, rows)
    return (place == jnp.arange(rows)[:, None]).astype(jnp.bfloat16)


def expert_kernel(blocks, where_ref, *refs):
    xs, refs = refs[: 2 * blocks], refs[2 * blocks :]
    pres, refs = [refs[2 * i : 2 * i + 2] for i in range(blocks)], refs[2 * blocks :]
    hbm, refs = refs[:4], refs[4:]
    outs, refs = refs[: 2 * blocks], refs[2 * blocks :]
    token_ref, down_ref, up_ref, sems = refs
    places = [down_ref.at[0], down_ref.at[1], up_ref.at[0], up_ref.at[1]]
    copies = [
        pltpu.make_async_copy(hbm[i], places[i], sems.at[i]) for i in range(len(places))
    ]
    for copy in copies:
        copy.start()
    width = outs[0].shape[1]
    chunk = 512 if width % 512 == 0 else 128
    expert = where_ref[0].astype(jnp.float32)
    slots = pres[0][0].shape[3]
    gates, placed = [], []
    for x_ref in xs:
        info = x_ref[:, width:].astype(jnp.float32)
        first = info[:, 0:1] == expert
        second = info[:, 1:2] == expert
        gates.append(jnp.where(first, info[:, 2:3], jnp.where(second, info[:, 3:4], 0.0)))
        slot = jnp.where(first, info[:, 4:5], jnp.where(second, info[:, 5:6], -1.0))
        column = lax.broadcasted_iota(jnp.int32, (x_ref.shape[0], slots), 1).astype(jnp.float32)
        placed.append(jnp.where(slot == column, 1.0, 0.0).astype(jnp.bfloat16))
    routed = []
    for start in range(0, width, chunk):
        routed.append(
            jnp.concatenate(
                [
                    x_ref[:, start : start + chunk].astype(jnp.float32) * gate
                    for x_ref, gate in zip(xs, gates)
                ],
                axis=0,
            ).astype(jnp.bfloat16)
        )
    across = (((1,), (1,)), ((), ()))
    pre_grads = []
    for j in range(2):
        preact = jnp.concatenate(
            [
                jnp.dot(
                    placed[i], pres[i // 2][j][0, i % 2, 0], preferred_element_type=jnp.float32
                )
                for i in range(2 * blocks)
            ],
            axis=0,
        )
        logistic = jax.nn.sigmoid(preact)
        factor = logistic * (1.0 + preact * (1.0 - logistic))
        copies[j].wait()
        hidden = jnp.zeros(factor.shape, jnp.float32)
        for k, part in enumerate(routed):
            hidden = hidden + lax.dot_general(
                part,
                down_ref[j, :, k * chunk : (k + 1) * chunk],
                across,
                preferred_element_type=jnp.float32,
            )
        pre_grads.append((hidden * factor).astype(jnp.bfloat16))
    copies[2].wait()
    copies[3].wait()
    for start in range(0, width, chunk):
        piece = sum(
            lax.dot_general(
                pre_grads[j],
                up_ref[j, start : start + chunk, :],
                across,
                preferred_element_type=jnp.float32,
            )
            for j in range(2)
        )
        row = 0
        for out_ref in outs:
            rows = out_ref.shape[0]
            out_ref[:, start : start + chunk] = piece[row : row + rows].astype(out_ref.dtype)
            row += rows
    token_ref[...] = jnp.zeros(token_ref.shape, token_ref.dtype)


def expert_rows(step_now, expert, origins, lanes_of, pres, downs, ups):
    blocks = len(origins)
    xs = [x for lanes in lanes_of for x in lanes]
    hidden, width = downs[0].shape
    _, lanes, _, slots, _ = pres[0].shape
    rows = sum(x.shape[0] for x in xs)

    def pre_block(i):
        return pl.BlockSpec(
            (1, lanes, 1, slots, hidden), lambda g, s: (step_now, 0, s[1 + i], 0, 0)
        )

    def whole(shape):
        return pl.BlockSpec(shape, lambda g, s: (0,) * len(shape))

    outs = [pltpu.HBM((x.shape[0], width), jnp.bfloat16) for x in xs]
    outs.append(pltpu.HBM((8, 128), jnp.float32))

    def in_hbm(arrays):
        return [pltpu.with_memory_space_constraint(array, pltpu.HBM) for array in arrays]

    *sums, token = pl.pallas_call(
        functools.partial(expert_kernel, blocks),
        out_shape=outs,
        grid_spec=pltpu.PrefetchScalarGridSpec(
            num_scalar_prefetch=1,
            grid=(1,),
            in_specs=[
                *[whole(x.shape) for x in xs],
                *[pre_block(i) for i in range(blocks) for _ in range(2)],
                *[pl.BlockSpec(memory_space=pl.ANY)] * 4,
            ],
            out_specs=[whole(out.shape) for out in outs],
            scratch_shapes=[
                pltpu.VMEM((2, hidden, width), jnp.bfloat16),
                pltpu.VMEM((2, width, hidden), jnp.bfloat16),
                pltpu.SemaphoreType.DMA((4,)),
            ],
        ),
        compiler_params=pltpu.CompilerParams(vmem_limit_bytes=48 * 1024 * 1024),
        cost_estimate=pl.CostEstimate(
            flops=8 * rows * hidden * width,
            bytes_accessed=8 * hidden * width + 4 * rows * width,
            transcendentals=2 * rows * hidden,
        ),
    )(
        jnp.stack([expert, *origins]).astype(jnp.int32),
        *in_hbm(xs),
        *in_hbm([pre for _ in range(blocks) for pre in pres]),
        *in_hbm([*downs, *ups]),
    )
    return [sums[2 * i : 2 * i + 2] for i in range(blocks)], token


def after(blocks, token):
    return [lax.optimization_barrier((block, token))[0] for block in blocks]


def add_rows(own, arrived):
    short = own.shape[0] - arrived.shape[0]
    arrived = jnp.pad(arrived.astype(jnp.float32), ((0, short), (0, 0)))
    return (own.astype(jnp.float32) + arrived).astype(jnp.bfloat16)


def body(grad_in, fresh_grad, routes, gate_weights, saved_pre, w_up, w_down):
    section_id = lax.axis_index("section")
    sections = lax.axis_size("section")
    groups = lax.axis_size("expert")
    device = lax.axis_index("expert")
    _, lanes, tokens, width = grad_in.shape
    chips, core = groups // 2, lax.rem(device, 2)
    chip, expert = lax.div(device, 2), lax.div(device, SLICES)
    experts = groups // SLICES
    capacity = saved_pre.shape[3] // groups
    half = chips // 2
    way = 1 - 2 * core
    outer = jnp.where(lax.rem(chip, 2) == 1 - core, 1, 0)
    first = lax.rem(experts + expert + way * (experts // 2 - 1 + outer), experts)
    second = lax.rem(experts + expert + way * (experts // 2 - 2 + outer), experts)
    sizes = [2 * tokens] * (half - 4) + [4 * capacity] * 2 + [2 * capacity] * 2

    def by_chip(block):
        return block.reshape(STEPS, lanes, chips, 2 * capacity, block.shape[-1])

    current = grad_in[0]
    weights = None
    for step_now in range(STEPS):
        info = row_info(routes[0, step_now], gate_weights[0, step_now], core * capacity)
        mine = jnp.concatenate([current, info], axis=-1)
        both = jnp.concatenate([mine, swap_cores(mine)], axis=1)
        sorting = sort_matrix(both[..., width:], capacity, first, second)
        payload = jnp.einsum(
            "kpr,krd->kpd", sorting, both, preferred_element_type=jnp.float32
        ).astype(jnp.bfloat16)

        def compute(blocks):
            origins, lanes_of = zip(*blocks)
            return expert_rows(step_now, expert, origins, lanes_of, *weights)

        streams = [payload[lane] for lane in range(lanes)]
        held, partials, token = [], [], None
        for distance, size in enumerate(sizes, 1):
            streams = [hop(s[:size], True, only=distance == half) for s in streams]
            if weights is None:
                saved, down, up, *_ = lax.optimization_barrier(
                    (saved_pre[0], w_down[0], w_up[0], *streams)
                )
                pres = [by_chip(saved), by_chip(swap_cores(saved))]
                weights = pres, [down, swap_cores(down)], [up, swap_cores(up)]
            if token is not None:
                streams, token = after(streams, token), None
            held.append((lax.rem(chips + chip - way * distance, chips), streams))
            if distance in (2, 4, 6):
                sums, token = compute(held)
                partials, held = partials + sums, []
        (own, before), token = compute([(chip, mine), held[0]])
        (last,), _ = compute([(held[1][0], after(held[1][1], token))])
        partials += [before, last]

        sums = partials[-1]
        for distance in range(half, 0, -1):
            sums = [hop(s, False, only=distance == half) for s in sums]
            if distance > 1:
                sums = [add_rows(o, s) for o, s in zip(partials[distance - 2], sums)]
        arrived = jnp.einsum(
            "kpr,kpd->krd", sorting, jnp.stack(sums), preferred_element_type=jnp.float32
        ).astype(jnp.bfloat16)
        crossed = swap_cores(arrived[:, tokens:])
        result = (
            current.astype(jnp.float32)
            + jnp.stack(own).astype(jnp.float32)
            + arrived[:, :tokens].astype(jnp.float32)
            + crossed.astype(jnp.float32)
        ).astype(jnp.bfloat16)
        if step_now + 1 < STEPS:
            from_above = from_behind(result[0], "section", -1)
            from_below = from_behind(result[1], "section", 1)
            toward_lower = jnp.where(section_id == sections - 1, fresh_grad[0], from_above)
            toward_higher = jnp.where(section_id == 0, fresh_grad[1], from_below)
            current = jnp.stack([toward_lower, toward_higher])
    return result[None]


def solution(mesh):
    placed = (
        P("section", None, "expert", None),
        P(None, "expert", None),
        P("section", None, None, "expert", None),
        P("section", None, None, "expert", None),
        P("section", None, None, None, "expert"),
        P("section", None, "expert"),
        P("section", "expert", None),
    )
    return jax.shard_map(
        body,
        mesh=mesh,
        in_specs=placed,
        out_specs=P("section", None, "expert", None),
        check_vma=False,
    )
```

```python
import functools

import jax
import jax.numpy as jnp
from jax import lax
from jax.experimental import pallas as pl
from jax.experimental.pallas import tpu as pltpu
from jax.sharding import PartitionSpec as P

SLICES = 4
STEPS = 2
INFO = 128
VMEM_LIMIT = 32 * 1024 * 1024


def from_behind(block, axis, distance):
    devices = range(lax.axis_size(axis))
    route = [(i - distance, i) for i in devices if i - distance in devices]
    return lax.ppermute(block, axis, route)


def swap_cores(block):
    devices = range(lax.axis_size("expert"))
    return lax.ppermute(block, "expert", [(i, i ^ 1) for i in devices])


def hop(block, outward, distance=1):
    devices = lax.axis_size("expert")
    chips = devices // 2
    route = []
    for i in range(devices):
        z, core = divmod(i, 2)
        way = 1 if core == 0 else -1
        target = (z + way * distance) % chips
        if distance == 2 and target // 2 != (z + way) % chips // 2:
            continue
        pair = (i, 2 * target + core)
        route.append(pair if outward else pair[::-1])
    return lax.ppermute(block, "expert", route)


def row_info(routes, gate_weights, first_slot):
    lanes, tokens, top = routes.shape
    experts = lax.axis_size("expert") // SLICES
    names = routes[..., None] == jnp.arange(experts, dtype=jnp.int32)
    chosen = jnp.sum(names.astype(jnp.int32), axis=2)
    rank = jnp.cumsum(chosen, axis=1) - chosen
    slots = jnp.sum(jnp.where(names, rank[:, :, None, :], 0), axis=-1) + first_slot
    info = jnp.concatenate(
        [routes.astype(jnp.bfloat16), gate_weights, slots.astype(jnp.bfloat16)], axis=-1
    )
    return jnp.pad(info, ((0, 0), (0, 0), (0, INFO - 3 * top)))


def sort_matrix(info, capacity, first, second):
    lanes, rows, _ = info.shape
    tokens = rows // 2
    ids = info[..., :2].astype(jnp.float32).reshape(lanes, 2, tokens, 2)
    key = jnp.where(
        jnp.any(ids == first, axis=-1), 0, jnp.where(jnp.any(ids == second, axis=-1), 1, 2)
    )
    order = key * tokens + jnp.arange(tokens)
    rank = jnp.sum((order[..., None, :] < order[..., :, None]).astype(jnp.int32), axis=-1)
    block = jnp.arange(2)[:, None]
    rest = tokens - 2 * capacity
    place = jnp.where(
        rank < capacity,
        block * capacity + rank,
        jnp.where(
            rank < 2 * capacity,
            2 * capacity + block * capacity + rank - capacity,
            4 * capacity + block * rest + rank - 2 * capacity,
        ),
    ).reshape(lanes, 1, rows)
    return (place == jnp.arange(rows)[:, None]).astype(jnp.bfloat16)


def expert_kernel(blocks, where_ref, *refs):
    xs, refs = refs[: 2 * blocks], refs[2 * blocks :]
    pres, (down_ref, up_ref), outs = refs[:blocks], refs[blocks : blocks + 2], refs[blocks + 2 :]
    width = outs[0].shape[1]
    chunk = 512 if width % 512 == 0 else 128
    expert = where_ref[0].astype(jnp.float32)
    slots = pres[0].shape[3]
    gates, placed = [], []
    for x_ref in xs:
        info = x_ref[:, width:].astype(jnp.float32)
        first = info[:, 0:1] == expert
        second = info[:, 1:2] == expert
        gates.append(jnp.where(first, info[:, 2:3], jnp.where(second, info[:, 3:4], 0.0)))
        slot = jnp.where(first, info[:, 4:5], jnp.where(second, info[:, 5:6], -1.0))
        column = lax.broadcasted_iota(jnp.int32, (x_ref.shape[0], slots), 1).astype(jnp.float32)
        placed.append(jnp.where(slot == column, 1.0, 0.0).astype(jnp.bfloat16))
    routed = []
    for start in range(0, width, chunk):
        routed.append(
            jnp.concatenate(
                [
                    x_ref[:, start : start + chunk].astype(jnp.float32) * gate
                    for x_ref, gate in zip(xs, gates)
                ],
                axis=0,
            ).astype(jnp.bfloat16)
        )
    across = (((1,), (1,)), ((), ()))
    preact = jnp.concatenate(
        [
            jnp.dot(placed[i], pres[i // 2][0, i % 2, 0], preferred_element_type=jnp.float32)
            for i in range(2 * blocks)
        ],
        axis=0,
    )
    logistic = jax.nn.sigmoid(preact)
    factor = logistic * (1.0 + preact * (1.0 - logistic))
    hidden = jnp.zeros(factor.shape, jnp.float32)
    for k, part in enumerate(routed):
        hidden = hidden + lax.dot_general(
            part,
            down_ref[:, k * chunk : (k + 1) * chunk],
            across,
            preferred_element_type=jnp.float32,
        )
    pre_grad = (hidden * factor).astype(jnp.bfloat16)
    for start in range(0, width, chunk):
        piece = lax.dot_general(
            pre_grad, up_ref[start : start + chunk, :], across, preferred_element_type=jnp.float32
        )
        row = 0
        for out_ref in outs:
            rows = out_ref.shape[0]
            out_ref[:, start : start + chunk] = piece[row : row + rows].astype(out_ref.dtype)
            row += rows


def expert_rows(step_now, expert, blocks, pre, down, up, wait_for=None):
    origins, lanes_of = zip(*blocks)
    xs = [x for lanes in lanes_of for x in lanes]
    hidden, width = down.shape
    _, lanes, _, slots, _ = pre.shape
    rows = sum(x.shape[0] for x in xs)
    once = pl.Buffered(1)
    scalars = jnp.stack([expert, *origins]).astype(jnp.int32)
    if wait_for is not None:
        scalars = lax.optimization_barrier((scalars, wait_for))[0]

    def pre_block(i):
        return pl.BlockSpec(
            (1, lanes, 1, slots, hidden), lambda g, s: (step_now, 0, s[1 + i], 0, 0)
        )

    def whole(shape):
        return pl.BlockSpec(shape, lambda g, s: (0,) * len(shape), pipeline_mode=once)

    outs = [jax.ShapeDtypeStruct((x.shape[0], width), jnp.bfloat16) for x in xs]
    sums = pl.pallas_call(
        functools.partial(expert_kernel, len(blocks)),
        out_shape=outs,
        grid_spec=pltpu.PrefetchScalarGridSpec(
            num_scalar_prefetch=1,
            grid=(1,),
            in_specs=[
                *[whole(x.shape) for x in xs],
                *[pre_block(i) for i in range(len(blocks))],
                whole(down.shape),
                whole(up.shape),
            ],
            out_specs=[whole(out.shape) for out in outs],
        ),
        compiler_params=pltpu.CompilerParams(vmem_limit_bytes=VMEM_LIMIT),
        cost_estimate=pl.CostEstimate(
            flops=4 * rows * hidden * width,
            bytes_accessed=4 * hidden * width + 4 * rows * width,
            transcendentals=rows * hidden,
        ),
    )(scalars, *xs, *[pre] * len(blocks), down, up)
    return [sums[2 * i : 2 * i + 2] for i in range(len(blocks))]


def add_rows(own, arrived):
    short = own.shape[0] - arrived.shape[0]
    arrived = jnp.pad(arrived.astype(jnp.float32), ((0, short), (0, 0)))
    return (own.astype(jnp.float32) + arrived).astype(jnp.bfloat16)


def body(grad_in, fresh_grad, routes, gate_weights, saved_pre, w_up, w_down):
    section_id = lax.axis_index("section")
    sections = lax.axis_size("section")
    groups = lax.axis_size("expert")
    device = lax.axis_index("expert")
    _, lanes, tokens, width = grad_in.shape
    chips, core = groups // 2, lax.rem(device, 2)
    chip, expert = lax.div(device, 2), lax.div(device, SLICES)
    experts = groups // SLICES
    capacity = saved_pre.shape[3] // groups
    half = chips // 2
    way = 1 - 2 * core
    outer = jnp.where(lax.rem(chip, 2) == 1 - core, 1, 0)
    first = lax.rem(experts + expert + way * (experts // 2 - 1 + outer), experts)
    second = lax.rem(experts + expert + way * (experts // 2 - 2 + outer), experts)
    sizes = [2 * tokens] * (half - 4) + [4 * capacity] * 2 + [2 * capacity] * 2

    pre = jnp.concatenate([saved_pre[0], swap_cores(saved_pre[0])], axis=-1)
    pre = pre.reshape(STEPS, lanes, chips, 2 * capacity, pre.shape[-1])
    down = jnp.concatenate([w_down[0], swap_cores(w_down[0])], axis=0)
    up = jnp.concatenate([w_up[0], swap_cores(w_up[0])], axis=1)
    current = grad_in[0]
    for step_now in range(STEPS):
        info = row_info(routes[0, step_now], gate_weights[0, step_now], core * capacity)
        mine = jnp.concatenate([current, info], axis=-1)
        both = jnp.concatenate([mine, swap_cores(mine)], axis=1)
        sorting = sort_matrix(both[..., width:], capacity, first, second)
        payload = jnp.einsum(
            "kpr,krd->kpd", sorting, both, preferred_element_type=jnp.float32
        ).astype(jnp.bfloat16)
        def compute(blocks, wait_for=None):
            return expert_rows(step_now, expert, blocks, pre, down, up, wait_for)

        streams = [payload[lane] for lane in range(lanes)]
        blocks = [(chip, mine)]
        for distance, size in enumerate(sizes, 1):
            far = distance == half
            arrived = [hop(s[:size], True, 2 if far else 1) for s in streams]
            blocks.append((lax.rem(chips + chip - way * distance, chips), arrived))
            if distance < half - 1:
                streams = arrived
        last = compute(blocks[half - 1 :])
        own, *late = compute([blocks[0], *blocks[half - 3 : half - 1]])
        sums = [
            add_rows(add_rows(o, hop(t, False)), hop(u, False, 2)) for o, t, u in zip(late[1], *last)
        ]
        partials = {half - 3: late[0]}
        for distance in range(half - 2, 0, -1):
            if distance - 1 not in partials and distance > 1:
                partials[distance - 2], partials[distance - 1] = compute(
                    blocks[distance - 2 : distance], sums[0]
                )
            sums = [hop(s, False) for s in sums]
            if distance > 1:
                sums = [add_rows(o, s) for o, s in zip(partials[distance - 1], sums)]
        arrived = jnp.einsum(
            "kpr,kpd->krd", sorting, jnp.stack(sums), preferred_element_type=jnp.float32
        ).astype(jnp.bfloat16)
        crossed = swap_cores(arrived[:, tokens:])
        result = (
            current.astype(jnp.float32)
            + jnp.stack(own).astype(jnp.float32)
            + arrived[:, :tokens].astype(jnp.float32)
            + crossed.astype(jnp.float32)
        ).astype(jnp.bfloat16)
        if step_now + 1 < STEPS:
            from_above = from_behind(result[0], "section", -1)
            from_below = from_behind(result[1], "section", 1)
            toward_lower = jnp.where(section_id == sections - 1, fresh_grad[0], from_above)
            toward_higher = jnp.where(section_id == 0, fresh_grad[1], from_below)
            current = jnp.stack([toward_lower, toward_higher])
    return result[None]


def solution(mesh):
    placed = (
        P("section", None, "expert", None),
        P(None, "expert", None),
        P("section", None, None, "expert", None),
        P("section", None, None, "expert", None),
        P("section", None, None, None, "expert"),
        P("section", None, "expert"),
        P("section", "expert", None),
    )
    return jax.shard_map(
        body,
        mesh=mesh,
        in_specs=placed,
        out_specs=P("section", None, "expert", None),
        check_vma=False,
    )
```

```python
import functools

import jax
import jax.numpy as jnp
from jax import lax
from jax.experimental import pallas as pl
from jax.experimental.pallas import tpu as pltpu
from jax.sharding import PartitionSpec as P

SLICES = 4
STEPS = 2
INFO = 128
VMEM_LIMIT = 22 * 1024 * 1024


def from_behind(block, axis, distance):
    devices = range(lax.axis_size(axis))
    route = [(i - distance, i) for i in devices if i - distance in devices]
    return lax.ppermute(block, axis, route)


def swap_cores(block):
    devices = range(lax.axis_size("expert"))
    return lax.ppermute(block, "expert", [(i, i ^ 1) for i in devices])


def hop(block, outward, distance=1):
    devices = lax.axis_size("expert")
    chips = devices // 2
    route = []
    for i in range(devices):
        z, core = divmod(i, 2)
        way = 1 if core == 0 else -1
        target = (z + way * distance) % chips
        if distance == 2 and target // 2 != (z + way) % chips // 2:
            continue
        pair = (i, 2 * target + core)
        route.append(pair if outward else pair[::-1])
    return lax.ppermute(block, "expert", route)


def row_info(routes, gate_weights, first_slot):
    lanes, tokens, top = routes.shape
    experts = lax.axis_size("expert") // SLICES
    names = routes[..., None] == jnp.arange(experts, dtype=jnp.int32)
    chosen = jnp.sum(names.astype(jnp.int32), axis=2)
    rank = jnp.cumsum(chosen, axis=1) - chosen
    slots = jnp.sum(jnp.where(names, rank[:, :, None, :], 0), axis=-1) + first_slot
    info = jnp.concatenate(
        [routes.astype(jnp.bfloat16), gate_weights, slots.astype(jnp.bfloat16)], axis=-1
    )
    return jnp.pad(info, ((0, 0), (0, 0), (0, INFO - 3 * top)))


def sort_matrix(info, first, second):
    lanes, rows, _ = info.shape
    tokens = rows // 2
    ids = info[..., :2].astype(jnp.float32).reshape(lanes, 2, tokens, 2)
    key = jnp.where(
        jnp.any(ids == first, axis=-1), 0, jnp.where(jnp.any(ids == second, axis=-1), 1, 2)
    )
    order = key * tokens + jnp.arange(tokens)
    rank = jnp.sum((order[..., None, :] < order[..., :, None]).astype(jnp.int32), axis=-1)
    place = (jnp.arange(2)[:, None] * tokens + rank).reshape(lanes, 1, rows)
    return (place == jnp.arange(rows)[:, None]).astype(jnp.bfloat16)


def expert_kernel(lane_of, origin_of, where_ref, *refs):
    xs, refs = refs[: len(lane_of)], refs[len(lane_of) :]
    outs, refs = refs[-len(lane_of) :], refs[: -len(lane_of)]
    *pres, down_ref, up_ref = refs
    width = outs[0].shape[1]
    chunk = 512 if width % 512 == 0 else 128
    expert = where_ref[0].astype(jnp.float32)
    slots = pres[0].shape[3]
    gates, placed = [], []
    for x_ref in xs:
        info = x_ref[:, width:].astype(jnp.float32)
        first = info[:, 0:1] == expert
        second = info[:, 1:2] == expert
        gates.append(jnp.where(first, info[:, 2:3], jnp.where(second, info[:, 3:4], 0.0)))
        slot = jnp.where(first, info[:, 4:5], jnp.where(second, info[:, 5:6], -1.0))
        column = lax.broadcasted_iota(jnp.int32, (x_ref.shape[0], slots), 1).astype(jnp.float32)
        placed.append(jnp.where(slot == column, 1.0, 0.0).astype(jnp.bfloat16))
    across = (((1,), (1,)), ((), ()))
    preact = jnp.concatenate(
        [
            jnp.dot(rows, pres[origin][0, lane, 0], preferred_element_type=jnp.float32)
            for rows, lane, origin in zip(placed, lane_of, origin_of)
        ],
        axis=0,
    )
    logistic = jax.nn.sigmoid(preact)
    factor = logistic * (1.0 + preact * (1.0 - logistic))
    hidden = jnp.zeros(factor.shape, jnp.float32)
    for start in range(0, width, chunk):
        routed = jnp.concatenate(
            [
                x_ref[:, start : start + chunk].astype(jnp.float32) * gate
                for x_ref, gate in zip(xs, gates)
            ],
            axis=0,
        ).astype(jnp.bfloat16)
        hidden = hidden + lax.dot_general(
            routed, down_ref[:, start : start + chunk], across, preferred_element_type=jnp.float32
        )
    pre_grad = (hidden * factor).astype(jnp.bfloat16)
    for start in range(0, width, chunk):
        piece = lax.dot_general(
            pre_grad, up_ref[start : start + chunk, :], across, preferred_element_type=jnp.float32
        )
        row = 0
        for out_ref in outs:
            rows = out_ref.shape[0]
            out_ref[:, start : start + chunk] = piece[row : row + rows].astype(out_ref.dtype)
            row += rows


def expert_rows(step_now, expert, blocks, pre, down, up, wait_for=None, in_hbm=()):
    origins = [origin for origin, _ in blocks]
    xs = [x for _, streams in blocks for x in streams]
    lane_of = [2 * i // len(streams) for _, streams in blocks for i in range(len(streams))]
    origin_of = [k for k, (_, streams) in enumerate(blocks) for _ in streams]
    hidden, width = down.shape
    _, lanes, _, slots, _ = pre.shape
    rows = sum(x.shape[0] for x in xs)
    once = pl.Buffered(1)
    scalars = jnp.stack([expert, *origins]).astype(jnp.int32)
    if wait_for is not None:
        scalars = lax.optimization_barrier((scalars, wait_for))[0]
        xs = [pltpu.with_memory_space_constraint(x, pltpu.HBM) for x in xs]

    def pre_block(i):
        return pl.BlockSpec(
            (1, lanes, 1, slots, hidden), lambda g, s: (step_now, 0, s[1 + i], 0, 0)
        )

    def whole(shape):
        return pl.BlockSpec(shape, lambda g, s: (0,) * len(shape), pipeline_mode=once)

    outs = [
        (pltpu.HBM if owner in in_hbm else jax.ShapeDtypeStruct)((x.shape[0], width), jnp.bfloat16)
        for x, owner in zip(xs, origin_of)
    ]
    sums = pl.pallas_call(
        functools.partial(expert_kernel, lane_of, origin_of),
        out_shape=outs,
        grid_spec=pltpu.PrefetchScalarGridSpec(
            num_scalar_prefetch=1,
            grid=(1,),
            in_specs=[
                *[whole(x.shape) for x in xs],
                *[pre_block(i) for i in range(len(blocks))],
                whole(down.shape),
                whole(up.shape),
            ],
            out_specs=[whole(out.shape) for out in outs],
        ),
        compiler_params=pltpu.CompilerParams(vmem_limit_bytes=VMEM_LIMIT),
        cost_estimate=pl.CostEstimate(
            flops=4 * rows * hidden * width,
            bytes_accessed=4 * hidden * width + 4 * rows * width,
            transcendentals=rows * hidden,
        ),
    )(scalars, *xs, *[pre] * len(blocks), down, up)
    return [
        [s for s, owner in zip(sums, origin_of) if owner == k] for k in range(len(blocks))
    ]


def add_rows(own, arrived):
    short = own.shape[0] - arrived.shape[0]
    arrived = jnp.pad(arrived.astype(jnp.float32), ((0, short), (0, 0)))
    return (own.astype(jnp.float32) + arrived).astype(jnp.bfloat16)


def body(grad_in, fresh_grad, routes, gate_weights, saved_pre, w_up, w_down):
    section_id = lax.axis_index("section")
    sections = lax.axis_size("section")
    groups = lax.axis_size("expert")
    device = lax.axis_index("expert")
    _, lanes, tokens, width = grad_in.shape
    chips, core = groups // 2, lax.rem(device, 2)
    chip, expert = lax.div(device, 2), lax.div(device, SLICES)
    experts = groups // SLICES
    capacity = saved_pre.shape[3] // groups
    half = chips // 2
    way = 1 - 2 * core
    outer = jnp.where(lax.rem(chip, 2) == 1 - core, 1, 0)
    first = lax.rem(experts + expert + way * (experts // 2 - 1 + outer), experts)
    second = lax.rem(experts + expert + way * (experts // 2 - 2 + outer), experts)
    sizes = [tokens] * (half - 4) + [2 * capacity] * 2

    pre = jnp.concatenate([saved_pre[0], swap_cores(saved_pre[0])], axis=-1)
    pre = pre.reshape(STEPS, lanes, chips, 2 * capacity, pre.shape[-1])
    down = jnp.concatenate([w_down[0], swap_cores(w_down[0])], axis=0)
    up = jnp.concatenate([w_up[0], swap_cores(w_up[0])], axis=1)
    current = grad_in[0]
    for step_now in range(STEPS):
        info = row_info(routes[0, step_now], gate_weights[0, step_now], core * capacity)
        mine = jnp.concatenate([current, info], axis=-1)
        both = jnp.concatenate([mine, swap_cores(mine)], axis=1)
        sorting = sort_matrix(both[..., width:], first, second)
        payload = jnp.einsum(
            "kpr,krd->kpd", sorting, both, preferred_element_type=jnp.float32
        ).astype(jnp.bfloat16)
        def compute(blocks, *how):
            return expert_rows(step_now, expert, blocks, pre, down, up, *how)

        def compute(blocks, *how):
            return expert_rows(step_now, expert, blocks, pre, down, up, *how)

        def origin(distance):
            return lax.rem(chips + chip - way * distance, chips)

        streams = [payload[i // 2, i % 2 * tokens :][:tokens] for i in range(2 * lanes)]
        blocks = [(chip, mine)]
        for distance, size in enumerate(sizes, 1):
            streams = [hop(s[:size], True) for s in streams]
            blocks.append((origin(distance), streams))
        streams = [
            jnp.concatenate([s[:capacity] for s in streams[2 * lane : 2 * lane + 2]], axis=0)
            for lane in range(lanes)
        ]
        for distance in (1, 2):
            arrived = [hop(s, True, distance) for s in streams]
            blocks.append((origin(half - 2 + distance), arrived))
        own, *partials, near, far = compute([blocks[0], *blocks[half - 3 :]], None, (0, 1, 2))
        sums = [add_rows(hop(t, False), hop(u, False, 2)) for t, u in zip(near, far)]
        sums = [s[b * capacity : (b + 1) * capacity] for s in sums for b in range(2)]
        sums = [add_rows(o, s) for o, s in zip(partials[1], sums)]
        partials = [None] * (half - 4) + partials
        for distance in range(half - 2, 0, -1):
            if distance == half - 3:
                partials[: half - 4] = compute(blocks[1 : half - 3], sums[0])
            sums = [hop(s, False) for s in sums]
            if distance > 1:
                sums = [add_rows(o, s) for o, s in zip(partials[distance - 2], sums)]
        sums = [jnp.concatenate(sums[2 * lane : 2 * lane + 2], axis=0) for lane in range(lanes)]
        arrived = jnp.einsum(
            "kpr,kpd->krd", sorting, jnp.stack(sums), preferred_element_type=jnp.float32
        ).astype(jnp.bfloat16)
        crossed = swap_cores(arrived[:, tokens:])
        result = (
            current.astype(jnp.float32)
            + jnp.stack(own).astype(jnp.float32)
            + arrived[:, :tokens].astype(jnp.float32)
            + crossed.astype(jnp.float32)
        ).astype(jnp.bfloat16)
        if step_now + 1 < STEPS:
            from_above = from_behind(result[0], "section", -1)
            from_below = from_behind(result[1], "section", 1)
            toward_lower = jnp.where(section_id == sections - 1, fresh_grad[0], from_above)
            toward_higher = jnp.where(section_id == 0, fresh_grad[1], from_below)
            current = jnp.stack([toward_lower, toward_higher])
    return result[None]


def solution(mesh):
    placed = (
        P("section", None, "expert", None),
        P(None, "expert", None),
        P("section", None, None, "expert", None),
        P("section", None, None, "expert", None),
        P("section", None, None, None, "expert"),
        P("section", None, "expert"),
        P("section", "expert", None),
    )
    return jax.shard_map(
        body,
        mesh=mesh,
        in_specs=placed,
        out_specs=P("section", None, "expert", None),
        check_vma=False,
    )
```

```python
import functools

import jax
import jax.numpy as jnp
from jax import lax
from jax.experimental import pallas as pl
from jax.experimental.pallas import tpu as pltpu
from jax.sharding import PartitionSpec as P

SLICES = 4
STEPS = 2
INFO = 128
VMEM_LIMIT = 32 * 1024 * 1024


def from_behind(block, axis, distance):
    devices = range(lax.axis_size(axis))
    route = [(i - distance, i) for i in devices if i - distance in devices]
    return lax.ppermute(block, axis, route)


def swap_cores(block):
    devices = range(lax.axis_size("expert"))
    return lax.ppermute(block, "expert", [(i, i ^ 1) for i in devices])


def hop(block, outward, distance=1):
    devices = lax.axis_size("expert")
    chips = devices // 2
    route = []
    for i in range(devices):
        z, core = divmod(i, 2)
        way = 1 if core == 0 else -1
        target = (z + way * distance) % chips
        if distance == 2 and target // 2 != (z + way) % chips // 2:
            continue
        pair = (i, 2 * target + core)
        route.append(pair if outward else pair[::-1])
    return lax.ppermute(block, "expert", route)


def row_info(routes, gate_weights, first_slot):
    lanes, tokens, top = routes.shape
    experts = lax.axis_size("expert") // SLICES
    names = routes[..., None] == jnp.arange(experts, dtype=jnp.int32)
    chosen = jnp.sum(names.astype(jnp.int32), axis=2)
    rank = jnp.cumsum(chosen, axis=1) - chosen
    slots = jnp.sum(jnp.where(names, rank[:, :, None, :], 0), axis=-1) + first_slot
    info = jnp.concatenate(
        [routes.astype(jnp.bfloat16), gate_weights, slots.astype(jnp.bfloat16)], axis=-1
    )
    return jnp.pad(info, ((0, 0), (0, 0), (0, INFO - 3 * top)))


def sort_matrix(info, capacity, first, second):
    lanes, rows, _ = info.shape
    tokens = rows // 2
    ids = info[..., :2].astype(jnp.float32).reshape(lanes, 2, tokens, 2)
    key = jnp.where(
        jnp.any(ids == first, axis=-1), 0, jnp.where(jnp.any(ids == second, axis=-1), 1, 2)
    )
    order = key * tokens + jnp.arange(tokens)
    rank = jnp.sum((order[..., None, :] < order[..., :, None]).astype(jnp.int32), axis=-1)
    block = jnp.arange(2)[:, None]
    rest = tokens - 2 * capacity
    place = jnp.where(
        rank < capacity,
        block * capacity + rank,
        jnp.where(
            rank < 2 * capacity,
            2 * capacity + block * capacity + rank - capacity,
            4 * capacity + block * rest + rank - 2 * capacity,
        ),
    ).reshape(lanes, 1, rows)
    return (place == jnp.arange(rows)[:, None]).astype(jnp.bfloat16)


def expert_kernel(blocks, where_ref, *refs):
    xs, refs = refs[: 2 * blocks], refs[2 * blocks :]
    pres, (down_ref, up_ref), outs = refs[:blocks], refs[blocks : blocks + 2], refs[blocks + 2 :]
    width = outs[0].shape[1]
    chunk = 512 if width % 512 == 0 else 128
    expert = where_ref[0].astype(jnp.float32)
    slots = pres[0].shape[3]
    gates, placed = [], []
    for x_ref in xs:
        info = x_ref[:, width:].astype(jnp.float32)
        first = info[:, 0:1] == expert
        second = info[:, 1:2] == expert
        gates.append(jnp.where(first, info[:, 2:3], jnp.where(second, info[:, 3:4], 0.0)))
        slot = jnp.where(first, info[:, 4:5], jnp.where(second, info[:, 5:6], -1.0))
        column = lax.broadcasted_iota(jnp.int32, (x_ref.shape[0], slots), 1).astype(jnp.float32)
        placed.append(jnp.where(slot == column, 1.0, 0.0).astype(jnp.bfloat16))
    routed = []
    for start in range(0, width, chunk):
        routed.append(
            jnp.concatenate(
                [
                    x_ref[:, start : start + chunk].astype(jnp.float32) * gate
                    for x_ref, gate in zip(xs, gates)
                ],
                axis=0,
            ).astype(jnp.bfloat16)
        )
    across = (((1,), (1,)), ((), ()))
    preact = jnp.concatenate(
        [
            jnp.dot(placed[i], pres[i // 2][0, i % 2, 0], preferred_element_type=jnp.float32)
            for i in range(2 * blocks)
        ],
        axis=0,
    )
    logistic = jax.nn.sigmoid(preact)
    factor = logistic * (1.0 + preact * (1.0 - logistic))
    hidden = jnp.zeros(factor.shape, jnp.float32)
    for k, part in enumerate(routed):
        hidden = hidden + lax.dot_general(
            part,
            down_ref[:, k * chunk : (k + 1) * chunk],
            across,
            preferred_element_type=jnp.float32,
        )
    pre_grad = (hidden * factor).astype(jnp.bfloat16)
    for start in range(0, width, chunk):
        piece = lax.dot_general(
            pre_grad, up_ref[start : start + chunk, :], across, preferred_element_type=jnp.float32
        )
        row = 0
        for out_ref in outs:
            rows = out_ref.shape[0]
            out_ref[:, start : start + chunk] = piece[row : row + rows].astype(out_ref.dtype)
            row += rows


def expert_rows(step_now, expert, blocks, pre, down, up, wait_for=None, in_hbm=True):
    origins, lanes_of = zip(*blocks)
    xs = [x for lanes in lanes_of for x in lanes]
    hidden, width = down.shape
    _, lanes, _, slots, _ = pre.shape
    rows = sum(x.shape[0] for x in xs)
    once = pl.Buffered(1)
    scalars = jnp.stack([expert, *origins]).astype(jnp.int32)
    if wait_for is not None:
        scalars = lax.optimization_barrier((scalars, wait_for))[0]

    def pre_block(i):
        return pl.BlockSpec(
            (1, lanes, 1, slots, hidden), lambda g, s: (step_now, 0, s[1 + i], 0, 0)
        )

    def whole(shape):
        return pl.BlockSpec(shape, lambda g, s: (0,) * len(shape), pipeline_mode=once)

    kind = pltpu.HBM if in_hbm else jax.ShapeDtypeStruct
    outs = [kind((x.shape[0], width), jnp.bfloat16) for x in xs]
    sums = pl.pallas_call(
        functools.partial(expert_kernel, len(blocks)),
        out_shape=outs,
        grid_spec=pltpu.PrefetchScalarGridSpec(
            num_scalar_prefetch=1,
            grid=(1,),
            in_specs=[
                *[whole(x.shape) for x in xs],
                *[pre_block(i) for i in range(len(blocks))],
                whole(down.shape),
                whole(up.shape),
            ],
            out_specs=[whole(out.shape) for out in outs],
        ),
        compiler_params=pltpu.CompilerParams(vmem_limit_bytes=VMEM_LIMIT),
        cost_estimate=pl.CostEstimate(
            flops=4 * rows * hidden * width,
            bytes_accessed=4 * hidden * width + 4 * rows * width,
            transcendentals=rows * hidden,
        ),
    )(scalars, *xs, *[pre] * len(blocks), down, up)
    return [sums[2 * i : 2 * i + 2] for i in range(len(blocks))]


def after(blocks, sums):
    return [lax.optimization_barrier((block, sums))[0] for block in blocks]


def add_rows(own, arrived):
    short = own.shape[0] - arrived.shape[0]
    arrived = jnp.pad(arrived.astype(jnp.float32), ((0, short), (0, 0)))
    return (own.astype(jnp.float32) + arrived).astype(jnp.bfloat16)


def body(grad_in, fresh_grad, routes, gate_weights, saved_pre, w_up, w_down):
    section_id = lax.axis_index("section")
    sections = lax.axis_size("section")
    groups = lax.axis_size("expert")
    device = lax.axis_index("expert")
    _, lanes, tokens, width = grad_in.shape
    chips, core = groups // 2, lax.rem(device, 2)
    chip, expert = lax.div(device, 2), lax.div(device, SLICES)
    experts = groups // SLICES
    capacity = saved_pre.shape[3] // groups
    half = chips // 2
    way = 1 - 2 * core
    outer = jnp.where(lax.rem(chip, 2) == 1 - core, 1, 0)
    first = lax.rem(experts + expert + way * (experts // 2 - 1 + outer), experts)
    second = lax.rem(experts + expert + way * (experts // 2 - 2 + outer), experts)
    sizes = [2 * tokens] * (half - 4) + [4 * capacity] * 2 + [2 * capacity] * 2

    pre = jnp.concatenate([saved_pre[0], swap_cores(saved_pre[0])], axis=-1)
    pre = pre.reshape(STEPS, lanes, chips, 2 * capacity, pre.shape[-1])
    down = jnp.concatenate([w_down[0], swap_cores(w_down[0])], axis=0)
    up = jnp.concatenate([w_up[0], swap_cores(w_up[0])], axis=1)
    current = grad_in[0]
    for step_now in range(STEPS):
        info = row_info(routes[0, step_now], gate_weights[0, step_now], core * capacity)
        mine = jnp.concatenate([current, info], axis=-1)
        both = jnp.concatenate([mine, swap_cores(mine)], axis=1)
        sorting = sort_matrix(both[..., width:], capacity, first, second)
        payload = jnp.einsum(
            "kpr,krd->kpd", sorting, both, preferred_element_type=jnp.float32
        ).astype(jnp.bfloat16)
        def compute(blocks, *how):
            return expert_rows(step_now, expert, blocks, pre, down, up, *how)

        ends = (half - 3, half - 2) if step_now == 0 else (half - 5, half - 3)
        streams = [payload[lane] for lane in range(lanes)]
        blocks, partials = [], []
        for distance, size in enumerate(sizes, 1):
            far = distance == half
            arrived = [hop(s[:size], True, 2 if far else 1) for s in streams]
            blocks.append((lax.rem(chips + chip - way * distance, chips), arrived))
            if distance in ends:
                first_block = len(partials)
                partials += compute(blocks[first_block : first_block + 2])
                arrived = after(arrived, partials[-1][1])
            if distance < half - 1:
                streams = arrived
        own, *late = compute([(chip, mine), *blocks[half - 4 : half - 2]])
        partials += late
        last = compute(blocks[half - 2 :], own[0], False)
        sums = [
            add_rows(add_rows(o, hop(t, False)), hop(u, False, 2))
            for o, t, u in zip(partials[-1], *last)
        ]
        for distance in range(half - 2, 0, -1):
            sums = [hop(s, False) for s in sums]
            if distance > 1:
                sums = [add_rows(o, s) for o, s in zip(partials[distance - 2], sums)]
        arrived = jnp.einsum(
            "kpr,kpd->krd", sorting, jnp.stack(sums), preferred_element_type=jnp.float32
        ).astype(jnp.bfloat16)
        crossed = swap_cores(arrived[:, tokens:])
        result = (
            current.astype(jnp.float32)
            + jnp.stack(own).astype(jnp.float32)
            + arrived[:, :tokens].astype(jnp.float32)
            + crossed.astype(jnp.float32)
        ).astype(jnp.bfloat16)
        if step_now + 1 < STEPS:
            from_above = from_behind(result[0], "section", -1)
            from_below = from_behind(result[1], "section", 1)
            toward_lower = jnp.where(section_id == sections - 1, fresh_grad[0], from_above)
            toward_higher = jnp.where(section_id == 0, fresh_grad[1], from_below)
            current = jnp.stack([toward_lower, toward_higher])
    return result[None]


def solution(mesh):
    placed = (
        P("section", None, "expert", None),
        P(None, "expert", None),
        P("section", None, None, "expert", None),
        P("section", None, None, "expert", None),
        P("section", None, None, None, "expert"),
        P("section", None, "expert"),
        P("section", "expert", None),
    )
    return jax.shard_map(
        body,
        mesh=mesh,
        in_specs=placed,
        out_specs=P("section", None, "expert", None),
        check_vma=False,
    )
```

```python
import functools

import jax
import jax.numpy as jnp
from jax import lax
from jax.experimental import pallas as pl
from jax.experimental.pallas import tpu as pltpu
from jax.sharding import PartitionSpec as P

SLICES = 4
STEPS = 2
INFO = 128
VMEM_LIMIT = 32 * 1024 * 1024


def from_behind(block, axis, distance):
    devices = range(lax.axis_size(axis))
    route = [(i - distance, i) for i in devices if i - distance in devices]
    return lax.ppermute(block, axis, route)


def swap_cores(block):
    devices = range(lax.axis_size("expert"))
    return lax.ppermute(block, "expert", [(i, i ^ 1) for i in devices])


def hop(block, outward, distance=1):
    devices = lax.axis_size("expert")
    chips = devices // 2
    route = []
    for i in range(devices):
        z, core = divmod(i, 2)
        way = 1 if core == 0 else -1
        target = (z + way * distance) % chips
        if distance == 2 and target // 2 != (z + way) % chips // 2:
            continue
        pair = (i, 2 * target + core)
        route.append(pair if outward else pair[::-1])
    return lax.ppermute(block, "expert", route)


def row_info(routes, gate_weights, first_slot):
    lanes, tokens, top = routes.shape
    experts = lax.axis_size("expert") // SLICES
    names = routes[..., None] == jnp.arange(experts, dtype=jnp.int32)
    chosen = jnp.sum(names.astype(jnp.int32), axis=2)
    rank = jnp.cumsum(chosen, axis=1) - chosen
    slots = jnp.sum(jnp.where(names, rank[:, :, None, :], 0), axis=-1) + first_slot
    info = jnp.concatenate(
        [routes.astype(jnp.bfloat16), gate_weights, slots.astype(jnp.bfloat16)], axis=-1
    )
    return jnp.pad(info, ((0, 0), (0, 0), (0, INFO - 3 * top)))


def sort_matrix(info, capacity, first, second):
    lanes, rows, _ = info.shape
    tokens = rows // 2
    ids = info[..., :2].astype(jnp.float32).reshape(lanes, 2, tokens, 2)
    key = jnp.where(
        jnp.any(ids == first, axis=-1), 0, jnp.where(jnp.any(ids == second, axis=-1), 1, 2)
    )
    order = key * tokens + jnp.arange(tokens)
    rank = jnp.sum((order[..., None, :] < order[..., :, None]).astype(jnp.int32), axis=-1)
    block = jnp.arange(2)[:, None]
    rest = tokens - 2 * capacity
    place = jnp.where(
        rank < capacity,
        block * capacity + rank,
        jnp.where(
            rank < 2 * capacity,
            2 * capacity + block * capacity + rank - capacity,
            4 * capacity + block * rest + rank - 2 * capacity,
        ),
    ).reshape(lanes, 1, rows)
    return (place == jnp.arange(rows)[:, None]).astype(jnp.bfloat16)


def expert_kernel(blocks, where_ref, *refs):
    xs, refs = refs[: 2 * blocks], refs[2 * blocks :]
    pres, (down_ref, up_ref), outs = refs[:blocks], refs[blocks : blocks + 2], refs[blocks + 2 :]
    width = outs[0].shape[1]
    chunk = 512 if width % 512 == 0 else 128
    expert = where_ref[0].astype(jnp.float32)
    slots = pres[0].shape[3]
    gates, placed = [], []
    for x_ref in xs:
        info = x_ref[:, width:].astype(jnp.float32)
        first = info[:, 0:1] == expert
        second = info[:, 1:2] == expert
        gates.append(jnp.where(first, info[:, 2:3], jnp.where(second, info[:, 3:4], 0.0)))
        slot = jnp.where(first, info[:, 4:5], jnp.where(second, info[:, 5:6], -1.0))
        column = lax.broadcasted_iota(jnp.int32, (x_ref.shape[0], slots), 1).astype(jnp.float32)
        placed.append(jnp.where(slot == column, 1.0, 0.0).astype(jnp.bfloat16))
    routed = []
    for start in range(0, width, chunk):
        routed.append(
            jnp.concatenate(
                [
                    x_ref[:, start : start + chunk].astype(jnp.float32) * gate
                    for x_ref, gate in zip(xs, gates)
                ],
                axis=0,
            ).astype(jnp.bfloat16)
        )
    across = (((1,), (1,)), ((), ()))
    preact = jnp.concatenate(
        [
            jnp.dot(placed[i], pres[i // 2][0, i % 2, 0], preferred_element_type=jnp.float32)
            for i in range(2 * blocks)
        ],
        axis=0,
    )
    logistic = jax.nn.sigmoid(preact)
    factor = logistic * (1.0 + preact * (1.0 - logistic))
    hidden = jnp.zeros(factor.shape, jnp.float32)
    for k, part in enumerate(routed):
        hidden = hidden + lax.dot_general(
            part,
            down_ref[:, k * chunk : (k + 1) * chunk],
            across,
            preferred_element_type=jnp.float32,
        )
    pre_grad = (hidden * factor).astype(jnp.bfloat16)
    for start in range(0, width, chunk):
        piece = lax.dot_general(
            pre_grad, up_ref[start : start + chunk, :], across, preferred_element_type=jnp.float32
        )
        row = 0
        for out_ref in outs:
            rows = out_ref.shape[0]
            out_ref[:, start : start + chunk] = piece[row : row + rows].astype(out_ref.dtype)
            row += rows


def expert_rows(step_now, expert, blocks, pre, down, up, wait_for=None):
    origins, lanes_of = zip(*blocks)
    xs = [x for lanes in lanes_of for x in lanes]
    hidden, width = down.shape
    _, lanes, _, slots, _ = pre.shape
    rows = sum(x.shape[0] for x in xs)
    once = pl.Buffered(1)
    scalars = jnp.stack([expert, *origins]).astype(jnp.int32)
    if wait_for is not None:
        scalars = lax.optimization_barrier((scalars, wait_for))[0]

    def pre_block(i):
        return pl.BlockSpec(
            (1, lanes, 1, slots, hidden), lambda g, s: (step_now, 0, s[1 + i], 0, 0)
        )

    def whole(shape):
        return pl.BlockSpec(shape, lambda g, s: (0,) * len(shape), pipeline_mode=once)

    kind = pltpu.HBM if step_now else jax.ShapeDtypeStruct
    outs = [kind((x.shape[0], width), jnp.bfloat16) for x in xs]
    sums = pl.pallas_call(
        functools.partial(expert_kernel, len(blocks)),
        out_shape=outs,
        grid_spec=pltpu.PrefetchScalarGridSpec(
            num_scalar_prefetch=1,
            grid=(1,),
            in_specs=[
                *[whole(x.shape) for x in xs],
                *[pre_block(i) for i in range(len(blocks))],
                whole(down.shape),
                whole(up.shape),
            ],
            out_specs=[whole(out.shape) for out in outs],
        ),
        compiler_params=pltpu.CompilerParams(vmem_limit_bytes=VMEM_LIMIT),
        cost_estimate=pl.CostEstimate(
            flops=4 * rows * hidden * width,
            bytes_accessed=4 * hidden * width + 4 * rows * width,
            transcendentals=rows * hidden,
        ),
    )(scalars, *xs, *[pre] * len(blocks), down, up)
    return [sums[2 * i : 2 * i + 2] for i in range(len(blocks))]


def after(blocks, sums):
    return [lax.optimization_barrier((block, sums))[0] for block in blocks]


def add_rows(own, arrived):
    short = own.shape[0] - arrived.shape[0]
    arrived = jnp.pad(arrived.astype(jnp.float32), ((0, short), (0, 0)))
    return (own.astype(jnp.float32) + arrived).astype(jnp.bfloat16)


def body(grad_in, fresh_grad, routes, gate_weights, saved_pre, w_up, w_down):
    section_id = lax.axis_index("section")
    sections = lax.axis_size("section")
    groups = lax.axis_size("expert")
    device = lax.axis_index("expert")
    _, lanes, tokens, width = grad_in.shape
    chips, core = groups // 2, lax.rem(device, 2)
    chip, expert = lax.div(device, 2), lax.div(device, SLICES)
    experts = groups // SLICES
    capacity = saved_pre.shape[3] // groups
    half = chips // 2
    way = 1 - 2 * core
    outer = jnp.where(lax.rem(chip, 2) == 1 - core, 1, 0)
    first = lax.rem(experts + expert + way * (experts // 2 - 1 + outer), experts)
    second = lax.rem(experts + expert + way * (experts // 2 - 2 + outer), experts)
    sizes = [2 * tokens] * (half - 4) + [4 * capacity] * 2 + [2 * capacity] * 2

    pre = jnp.concatenate([saved_pre[0], swap_cores(saved_pre[0])], axis=-1)
    pre = pre.reshape(STEPS, lanes, chips, 2 * capacity, pre.shape[-1])
    down = jnp.concatenate([w_down[0], swap_cores(w_down[0])], axis=0)
    up = jnp.concatenate([w_up[0], swap_cores(w_up[0])], axis=1)
    current = grad_in[0]
    for step_now in range(STEPS):
        info = row_info(routes[0, step_now], gate_weights[0, step_now], core * capacity)
        mine = jnp.concatenate([current, info], axis=-1)
        both = jnp.concatenate([mine, swap_cores(mine)], axis=1)
        sorting = sort_matrix(both[..., width:], capacity, first, second)
        payload = jnp.einsum(
            "kpr,krd->kpd", sorting, both, preferred_element_type=jnp.float32
        ).astype(jnp.bfloat16)
        def compute(blocks, wait_for=None):
            return expert_rows(step_now, expert, blocks, pre, down, up, wait_for)

        ends = () if step_now == 0 else (half - 5, half - 3)
        streams = [payload[lane] for lane in range(lanes)]
        blocks, partials = [(chip, mine)], []
        for distance, size in enumerate(sizes, 1):
            far = distance == half
            arrived = [hop(s[:size], True, 2 if far else 1) for s in streams]
            blocks.append((lax.rem(chips + chip - way * distance, chips), arrived))
            if distance in ends:
                done = len(partials)
                partials += compute(blocks[done : done + (2 if done else 3)])
                arrived = after(arrived, partials[-1][1])
            if distance < half - 1:
                streams = arrived
        partials = partials or [None] * (half - 3)
        partials += compute(blocks[half - 3 :])
        sums = [
            add_rows(add_rows(o, hop(t, False)), hop(u, False, 2))
            for o, t, u in zip(*partials[half - 2 :])
        ]
        for distance in range(half - 2, 0, -1):
            if distance > 1 and partials[distance - 1] is None:
                done = 3 * (distance // 4)
                partials[done:distance] = compute(blocks[done:distance], sums[0])
            sums = [hop(s, False) for s in sums]
            if distance > 1:
                sums = [add_rows(o, s) for o, s in zip(partials[distance - 1], sums)]
        own = partials[0]
        arrived = jnp.einsum(
            "kpr,kpd->krd", sorting, jnp.stack(sums), preferred_element_type=jnp.float32
        ).astype(jnp.bfloat16)
        crossed = swap_cores(arrived[:, tokens:])
        result = (
            current.astype(jnp.float32)
            + jnp.stack(own).astype(jnp.float32)
            + arrived[:, :tokens].astype(jnp.float32)
            + crossed.astype(jnp.float32)
        ).astype(jnp.bfloat16)
        if step_now + 1 < STEPS:
            from_above = from_behind(result[0], "section", -1)
            from_below = from_behind(result[1], "section", 1)
            toward_lower = jnp.where(section_id == sections - 1, fresh_grad[0], from_above)
            toward_higher = jnp.where(section_id == 0, fresh_grad[1], from_below)
            current = jnp.stack([toward_lower, toward_higher])
    return result[None]


def solution(mesh):
    placed = (
        P("section", None, "expert", None),
        P(None, "expert", None),
        P("section", None, None, "expert", None),
        P("section", None, None, "expert", None),
        P("section", None, None, None, "expert"),
        P("section", None, "expert"),
        P("section", "expert", None),
    )
    return jax.shard_map(
        body,
        mesh=mesh,
        in_specs=placed,
        out_specs=P("section", None, "expert", None),
        check_vma=False,
    )
```
